32 devices in a mesh: ens: 1, wide: 16 (over z, y, x), lev: 2 (over core).
Axes of the slice: x: 2, y: 2, z: 4, core: 2. Of those that a mesh axis runs over, the one named last changes fastest.
Arguments:
- model_state: float32 [4, 8, 128, 1024], P('ens', 'lev', 'wide'), may hold values from -6 to 6
- grid_points: int32 [128], P('wide'), may hold values from 32 to 1024, as said below
- quad_weights: float32 [128], P('wide'), may hold values from 0.5 to 2
- slot_waves: int32 [512], replicated, may hold values from 0 to 511, each once
- legendre: bfloat16 [512, 512, 128], P(('wide', 'lev')), may hold values from -0.5 to 0.5
- mode_in: float32 [8, 8], replicated, may hold values from -2 to 2
- mode_out: float32 [8, 8], replicated, may hold values from -2 to 2
- mode_rates: float32 [8], replicated, may hold values from 0.05 to 2
Outputs:
- new_state: float32 [4, 8, 128, 1024], P('ens', 'lev', 'wide')
- energy: float32 [8, 512], P('ens', ('wide', 'lev'))
The draws below stay inside these ranges and needn't reach their ends.
Inputs may be any that keep to these rules, and one draw needn't show every extreme that they name: `slot_waves`: each wavenumber is held by exactly one slot. `grid_points`: the two latitudes next to the equator have 1024 points.
All inputs are finite; a program needn't handle non-finite values.
Results may differ from the reference program's by a relative error of at most 0.0067.
Values may be sent and summed in bfloat16 or wider, within the bound.
A program may use at most 64 MiB of HBM per device.

```python
import math
import jax
import jax.numpy as jnp
from jax import lax

M1 = 512
NLON = 1024
L = 8
NLAT = 128
FIELDS = 4


def draw_grid_points(key, part):
    latitude = jnp.arange(NLAT, dtype=jnp.int32)
    from_pole = jnp.minimum(latitude, NLAT - 1 - latitude)
    jitter = jax.random.randint(key, (NLAT,), 0, 8).astype(jnp.int32)
    jitter = jnp.where(from_pole == 0, 0, jitter)
    return jnp.minimum(NLON, 16 + jitter + 2 * NLON * (from_pole + 1) // NLAT).astype(jnp.int32)


def shard_levels(own_key, shape, shards, least, largest):
    def one(dim, parts):
        steps = jax.random.uniform(jax.random.fold_in(jax.random.fold_in(own_key, 6), dim), (parts,), jnp.float32, least / len(shards), largest / len(shards))
        return jnp.repeat(jnp.exp(steps), shape[dim] // parts).reshape((-1,) + (1,) * (len(shape) - dim - 1))

    gain = one(*shards[0])
    for cut in shards[1:]:
        gain = gain * one(*cut)
    return gain


def bell_draw(rng, dims, spread, bound, cuts=(), kind=jnp.bfloat16):
    loudness = shard_levels(rng, dims, cuts, -0.22, 0.18) if cuts else 1.0
    values = jax.random.normal(rng, dims, jnp.float32) * spread * loudness
    return jnp.minimum(jnp.maximum(values, -bound), bound).astype(kind)


def setup_inputs(seed: int = 0, part: int = 0) -> dict:
    streams_of = jax.random.split(jax.random.key(seed), 9)
    part_keys = jax.random.split(jax.random.fold_in(streams_of[8], part), 9)
    model_state = bell_draw(part_keys[0], (FIELDS, L, NLAT, NLON), 1.0, 6.0, ((1, 2), (2, 16)), jnp.float32)
    grid_points = draw_grid_points(jax.random.fold_in(streams_of[8], 71), part)
    quad_weights = jnp.clip(jnp.exp(math.log(2.0) - 1.3862944 * jax.random.uniform(streams_of[2], (NLAT,), jnp.float32) ** shard_levels(streams_of[2], (NLAT,), ((0, 16),), -0.2, 0.2)), 0.5, 2.0)
    slot_waves = jax.random.permutation(streams_of[3], M1).astype(jnp.int32)
    legendre = bell_draw(streams_of[4], (M1, M1, NLAT), NLAT ** -0.5, 0.5, ((0, 32),))
    mode_in = bell_draw(streams_of[5], (L, L), L ** -0.5, 2.0, (), jnp.float32)
    mode_out = bell_draw(streams_of[6], (L, L), L ** -0.5, 2.0, (), jnp.float32)
    mode_rates = jnp.clip(jnp.exp(jax.random.uniform(streams_of[7], (L,), jnp.float32, math.log(0.05), math.log(2.0))), 0.05, 2.0)
    return dict(model_state=model_state, grid_points=grid_points, quad_weights=quad_weights, slot_waves=slot_waves, legendre=legendre, mode_in=mode_in, mode_out=mode_out, mode_rates=mode_rates)


def tendency(fields):
    diverge = fields[0]
    first = diverge - 0.25 * diverge * diverge
    others = fields[1:] - 0.25 * fields[1:] * diverge[None]
    return jnp.concatenate([first[None], others], axis=0)


def harmonic_tables(points, longitudes, wave_count, modes_axis):
    layout = (longitudes, wave_count) if modes_axis == 1 else (wave_count, longitudes)
    position = lax.broadcasted_iota(jnp.int32, layout, 1 - modes_axis)
    wavenum = lax.broadcasted_iota(jnp.int32, layout, modes_axis)
    phases = (wavenum * position) % points
    angles = phases.astype(jnp.float32) * (2.0 * math.pi / points.astype(jnp.float32))
    inside = (position < points) & (wavenum < (points + 1) // 2)
    cosine_part = jnp.where(inside, jnp.cos(angles), 0.0)
    sine_part = jnp.where(inside, jnp.sin(angles), 0.0)
    return cosine_part, sine_part, wavenum


def forward_lat(element):
    lat_block, points, weight = element
    cosine_part, sine_part, wavenum = harmonic_tables(points, NLON, M1, 1)
    tables = jnp.concatenate([cosine_part, -sine_part], axis=1).astype(jnp.bfloat16)
    row_block = lat_block.reshape(-1, NLON)
    fourier = jnp.dot(row_block.astype(jnp.float32), tables.astype(jnp.float32), preferred_element_type=jnp.float32)
    weighting = weight / points.astype(jnp.float32)
    return (fourier * weighting).astype(jnp.bfloat16).reshape(FIELDS, L, 2, M1)


def inverse_lat(element):
    coefficients, points = element
    cosine_part, sine_part, wavenum = harmonic_tables(points, NLON, M1, 0)
    factor = jnp.where(wavenum == 0, 1.0, 2.0)
    tables = jnp.concatenate([factor * cosine_part, -factor * sine_part], axis=0).astype(jnp.bfloat16)
    values = jnp.dot(coefficients.reshape(-1, 2 * M1).astype(jnp.float32), tables.astype(jnp.float32), preferred_element_type=jnp.float32)
    return tendency(values.reshape(FIELDS, L, NLON))


def implicit_step(spectral, mode_in, mode_out, mode_rates):
    slot_count = spectral.shape[0]
    blocks = spectral.reshape(slot_count, M1, L, FIELDS, 2)
    degree = jnp.arange(M1, dtype=jnp.float32)
    laplace = degree * (degree + 1.0) / (M1 * M1)
    laplace_four = laplace[None, :, None, None]
    highest = lax.Precision.HIGHEST
    diverge = blocks[:, :, :, 0, :]
    geopot = blocks[:, :, :, 1, :]
    tracer = blocks[:, :, :, 2:, :]
    div_modes = jnp.einsum('kl,snlc->snkc', mode_in, diverge, precision=highest)
    geo_modes = jnp.einsum('kl,snlc->snkc', mode_in, geopot, precision=highest)
    rate_grid = mode_rates[None, None, :, None]
    div_next = (div_modes + 2.0 * laplace_four * geo_modes) / (1.0 + 4.0 * laplace_four * rate_grid)
    geo_next = geo_modes - 2.0 * rate_grid * div_next
    div_level = jnp.einsum('lk,snkc->snlc', mode_out, div_next, precision=highest)
    geo_level = jnp.einsum('lk,snkc->snlc', mode_out, geo_next, precision=highest)
    tracer_next = tracer / (1.0 + 8.0 * laplace * laplace)[None, :, None, None, None]
    updated = jnp.concatenate([div_level[:, :, :, None, :], geo_level[:, :, :, None, :], tracer_next], axis=3)
    energy = jnp.einsum('snlc,snlc->ln', div_level, div_level, precision=highest) * (M1 / (degree + 1.0))[None, :]
    return updated.reshape(slot_count, M1, -1), energy


def reference(model_state, grid_points, quad_weights, slot_waves, legendre, mode_in, mode_out, mode_rates):
    explicit = tendency(model_state).astype(jnp.bfloat16)
    by_lat = jnp.transpose(explicit, (2, 0, 1, 3))
    fourier = lax.map(forward_lat, (by_lat, grid_points, quad_weights))
    ordered = jnp.take(fourier, slot_waves, axis=4)
    ordered = jnp.transpose(ordered, (4, 2, 1, 3, 0)).reshape(M1, L * FIELDS * 2, NLAT)
    degree = jnp.arange(M1, dtype=jnp.int32)

    def forward_slot(element):
        slot_table, slot_data, slot_wave = element
        result = jnp.dot(slot_table.astype(jnp.float32), slot_data.astype(jnp.float32).T, preferred_element_type=jnp.float32)
        return jnp.where((degree >= slot_wave)[:, None], result, 0.0)

    spectral = lax.map(forward_slot, (legendre, ordered, slot_waves))
    updated, energy = implicit_step(spectral, mode_in, mode_out, mode_rates)
    packed = updated.astype(jnp.bfloat16)

    def inverse_slot(element):
        slot_spec, slot_table = element
        result = jnp.dot(slot_spec.astype(jnp.float32).T, slot_table.astype(jnp.float32), preferred_element_type=jnp.float32)
        return result.astype(jnp.bfloat16)

    returned = lax.map(inverse_slot, (packed, legendre))
    slot_of = jnp.zeros((M1,), jnp.int32).at[slot_waves].set(jnp.arange(M1, dtype=jnp.int32))
    by_wave = jnp.take(returned, slot_of, axis=0)
    by_wave = by_wave.reshape(M1, L, FIELDS, 2, NLAT).transpose(4, 2, 1, 3, 0)
    gridded = lax.map(inverse_lat, (by_wave, grid_points))
    new_state = jnp.transpose(gridded, (1, 2, 0, 3))
    return new_state, energy
```

```python
from functools import partial
import math

import jax
import jax.numpy as jnp
from jax import lax
from jax.experimental import pallas as pl
from jax.experimental.pallas import tpu as pltpu
from jax.sharding import PartitionSpec as P

LANES = 128
PAD_SLOTS = 16
LATS = 8
VMEM = 40 * 1024 * 1024


def exchange(arrays, stride):
    lane = lax.broadcasted_iota(jnp.int32, arrays[0].shape, 1)
    arrays = list(arrays)
    step = 1
    while step < len(arrays):
        shift = step * stride
        upper = (lane & shift) != 0
        for low in range(len(arrays)):
            if low & step:
                continue
            first, second = arrays[low], arrays[low | step]
            arrays[low] = jnp.where(upper, pltpu.roll(second, shift, 1), first)
            arrays[low | step] = jnp.where(upper, second, pltpu.roll(first, LANES - shift, 1))
        step *= 2
    return arrays


def turn_pair(product, points, inverse):
    turns = jnp.floor(product * inverse + 0.5)
    half = (product - turns * points) * inverse * math.pi
    square = half * half
    cosine = 1.0 / 479001600.0
    for term in (-1.0 / 3628800.0, 1.0 / 40320.0, -1.0 / 720.0, 1.0 / 24.0, -0.5, 1.0):
        cosine = cosine * square + term
    sine = 1.0 / 6227020800.0
    for term in (-1.0 / 39916800.0, 1.0 / 362880.0, -1.0 / 5040.0, 1.0 / 120.0, -1.0 / 6.0, 1.0):
        sine = sine * square + term
    sine = sine * half
    return (1.0 - 2.0 * sine * sine, 2.0 * sine * cosine)


def fill_tables(points, inverse, cos_ref, sin_ref, base_ref):
    rows, lanes = cos_ref.shape
    highs = rows // 16
    row = lax.broadcasted_iota(jnp.int32, (16 + highs, lanes), 0)
    lane = lax.broadcasted_iota(jnp.int32, (16 + highs, lanes), 1)
    number = jnp.where(row < 16, row, (row - 16) * 16)
    cosine, sine = turn_pair((number * lane).astype(jnp.float32), points, inverse)
    base_ref[0] = cosine
    base_ref[1] = sine
    width = 256
    for start in range(0, lanes, width):
        cut = pl.ds(start, width)
        low_cos = base_ref[0, 0:16, cut]
        low_sin = base_ref[1, 0:16, cut]
        for high in range(highs):
            high_cos = base_ref[0, 16 + high : 17 + high, cut]
            high_sin = base_ref[1, 16 + high : 17 + high, cut]
            place = pl.ds(high * 16, 16)
            cos_ref[place, cut] = (high_cos * low_cos - high_sin * low_sin).astype(jnp.bfloat16)
            sin_ref[place, cut] = (high_sin * low_cos + high_cos * low_sin).astype(jnp.bfloat16)


def strided_rows(ref, start, count, stride):
    place = pl.ds(start, count, stride=stride) if stride else slice(None)
    return jnp.concatenate([ref[block, place, :] for block in range(ref.shape[0])], axis=1)


def store_strided(ref, start, count, stride, value):
    place = pl.ds(start, count, stride=stride)
    for block in range(ref.shape[0]):
        ref[block, place, :] = value[:, block * LANES : (block + 1) * LANES]


def tendency_tile(read, write, rows, fields):
    for start in range(0, rows // fields, 8):
        diverge = read(pl.ds(start, 8))
        for field in range(fields):
            place = pl.ds(field * (rows // fields) + start, 8)
            value = read(place)
            write(place, value - 0.25 * value * diverge)


def tendency_in(source, target, fields):
    for block in range(target.shape[0]):
        cut = pl.ds(block * LANES, LANES)

        def write(place, value):
            target[block, place, :] = value

        tendency_tile(lambda place: source[place, cut], write, source.shape[0], fields)


def tendency_out(source, target, fields):
    for block in range(source.shape[0]):
        cut = pl.ds(block * LANES, LANES)

        def write(place, value):
            target[place, cut] = value

        tendency_tile(lambda place: source[block, place, :], write, target.shape[0], fields)


def select_matrix(waves, wave_count):
    row = lax.broadcasted_iota(jnp.int32, (wave_count, waves.shape[1]), 0)
    return jnp.where(row == waves, 1.0, 0.0).astype(jnp.bfloat16)


def forward_kernel(
    fields, wave_count, points_ref, weight_ref, state_ref, waves_ref, out_ref,
    explicit, cos_ref, sin_ref, base_ref, rows_ref, moved,
):
    longitudes = state_ref.shape[1]
    series = state_ref.shape[0] // LATS
    comps = 2 * series
    tendency_in(state_ref, explicit, fields)
    position = lax.broadcasted_iota(jnp.int32, (series, longitudes), 1)
    wave = lax.broadcasted_iota(jnp.int32, (series, wave_count), 1)

    def one_lat(lat, carry):
        points = points_ref[lat]
        count = points.astype(jnp.float32)
        inverse = 1.0 / jnp.full((1, wave_count), count, jnp.float32)
        fill_tables(count, inverse, cos_ref, sin_ref, base_ref)
        data = strided_rows(explicit, lat, series, LATS)
        data = jnp.where(position < points, data, 0.0).astype(jnp.bfloat16)
        scale = jnp.where(wave < (points + 1) // 2, inverse * weight_ref[lat], 0.0)
        first = jnp.dot(data, cos_ref[...], preferred_element_type=jnp.float32)
        second = jnp.dot(data, sin_ref[...], preferred_element_type=jnp.float32)
        start = lat * comps
        store_strided(rows_ref, start, series, 2, first * scale)
        store_strided(rows_ref, start + 1, series, 2, -second * scale)
        return carry

    lax.fori_loop(0, LATS, one_lat, 0)
    select = select_matrix(waves_ref[...], wave_count)
    rows = strided_rows(rows_ref, 0, rows_ref.shape[1], None).astype(jnp.bfloat16)
    moved[...] = jnp.dot(rows, select, preferred_element_type=jnp.float32)
    for group in range(moved.shape[1] // LANES):
        cut = pl.ds(group * LANES, LANES)
        for start in range(0, comps, 16):
            arrays = exchange(
                [moved[pl.ds(lat * comps + start, 16), cut] for lat in range(LATS)], 1
            )
            for place, value in enumerate(arrays):
                out_ref[group * LATS + place, pl.ds(start, 16), :] = value.astype(jnp.bfloat16)


def mix_weights(matrix_ref, row):
    pairs = {}
    for target in range(2):
        for source in range(2):
            for shift in range(4):
                value = jnp.zeros(row.shape, jnp.float32)
                for mode in range(4):
                    scalar = matrix_ref[target * 4 + mode, source * 4 + (mode - shift) % 4]
                    value = jnp.where(row // 2 == mode, scalar, value)
                pairs[target, source, shift] = value
    return pairs


def mix(weights_ref, which, tiles):
    shifted = [
        [tile if shift == 0 else pltpu.roll(tile, 2 * shift, 0) for shift in range(4)]
        for tile in tiles
    ]
    results = []
    for target in range(2):
        total = None
        for source in range(2):
            for shift in range(4):
                weight = weights_ref[which * 16 + target * 8 + source * 4 + shift]
                term = weight * shifted[source][shift]
                total = term if total is None else total + term
        results.append(total)
    return results


def spectral_kernel(
    slots, waves_ref, mode_in_ref, mode_out_ref, rates_ref, got_ref, legendre_ref,
    out_ref, energy_ref, rows_ref, weights_ref, factor_ref, packed_ref, back_ref, total_ref,
):
    devices, comps = got_ref.shape[0], got_ref.shape[1]
    wide = devices // 2
    wave_count = legendre_ref.shape[1]
    device = lax.axis_index("wide") * 2 + lax.axis_index("lev")
    row = lax.broadcasted_iota(jnp.int32, (8, LANES), 0)
    for which, matrix_ref in enumerate((mode_in_ref, mode_out_ref)):
        for (target, source, shift), value in mix_weights(matrix_ref, row).items():
            weights_ref[which * 16 + target * 8 + source * 4 + shift] = value
    degree = lax.broadcasted_iota(jnp.int32, (8, wave_count), 1).astype(jnp.float32)
    laplace = degree * (degree + 1.0) / (wave_count * wave_count)
    wide_row = lax.broadcasted_iota(jnp.int32, (8, wave_count), 0)
    for target in range(2):
        rate = jnp.zeros((8, wave_count), jnp.float32)
        for mode in range(4):
            rate = jnp.where(wide_row // 2 == mode, rates_ref[target * 4 + mode], rate)
        factor_ref[target] = 1.0 / (1.0 + 4.0 * laplace * rate)
        factor_ref[2 + target] = 2.0 * rate
    factor_ref[4] = 2.0 * laplace
    factor_ref[5] = 1.0 / (1.0 + 8.0 * laplace * laplace)
    factor_ref[6] = wave_count / (degree + 1.0)
    total_ref[...] = jnp.zeros_like(total_ref)

    for lev in range(2):
        for start in range(0, comps, 16):
            place = pl.ds(lev * comps + start, 16)
            for group in range(wide // PAD_SLOTS):
                arrays = exchange(
                    [
                        got_ref[(group * PAD_SLOTS + w) * 2 + lev, pl.ds(start, 16), :].astype(
                            jnp.float32
                        )
                        for w in range(PAD_SLOTS)
                    ],
                    LATS,
                )
                for slot in range(slots):
                    rows_ref[slot, place, pl.ds(group * LANES, LANES)] = arrays[slot].astype(
                        jnp.bfloat16
                    )

    def one_slot(slot, carry):
        spectral = lax.dot_general(
            rows_ref[slot], legendre_ref[slot], (((1,), (1,)), ((), ())),
            preferred_element_type=jnp.float32,
        )
        own_wave = waves_ref[device * slots + slot]
        for start in range(0, wave_count, LANES):
            cut = pl.ds(start, LANES)
            lane = lax.broadcasted_iota(jnp.int32, (8, LANES), 1) + start
            kept = lane >= own_wave

            def tile(lev, index):
                first = lev * comps + index * 8
                return jnp.where(kept, spectral[first : first + 8, start : start + LANES], 0.0)

            div_modes = mix(weights_ref, 0, [tile(lev, 0) for lev in range(2)])
            geo_modes = mix(weights_ref, 0, [tile(lev, 1) for lev in range(2)])
            twice = factor_ref[4, :, cut]
            div_next = [
                (div_modes[lev] + twice * geo_modes[lev]) * factor_ref[lev, :, cut]
                for lev in range(2)
            ]
            geo_next = [
                geo_modes[lev] - factor_ref[2 + lev, :, cut] * div_next[lev] for lev in range(2)
            ]
            div_level = mix(weights_ref, 1, div_next)
            geo_level = mix(weights_ref, 1, geo_next)
            damp = factor_ref[5, :, cut]
            for lev in range(2):
                total_ref[lev, :, cut] += div_level[lev] * div_level[lev]
                tiles = [div_level[lev], geo_level[lev]] + [
                    tile(lev, index) * damp for index in range(2, comps // 8)
                ]
                for index in range(0, comps // 8, 2):
                    packed_ref[pl.ds(lev * comps + index * 8, 16), cut] = jnp.concatenate(
                        tiles[index : index + 2], axis=0
                    ).astype(jnp.bfloat16)
        back_ref[slot] = jnp.dot(
            packed_ref[...], legendre_ref[slot], preferred_element_type=jnp.float32
        )
        return carry

    lax.fori_loop(0, slots, one_slot, 0)

    for lev in range(2):
        for start in range(0, comps, 16):
            place = pl.ds(lev * comps + start, 16)
            for group in range(wide // PAD_SLOTS):
                arrays = exchange(
                    [
                        back_ref[slot, place, pl.ds(group * LANES, LANES)]
                        if slot < slots
                        else jnp.zeros((16, LANES), jnp.float32)
                        for slot in range(PAD_SLOTS)
                    ],
                    LATS,
                )
                for w in range(PAD_SLOTS):
                    out_ref[(group * PAD_SLOTS + w) * 2 + lev, pl.ds(start, 16), :] = arrays[
                        w
                    ].astype(jnp.bfloat16)

    share = wave_count // devices
    for start in range(0, wave_count, LANES):
        cut = pl.ds(start, LANES)
        first, second = total_ref[0, :, cut], total_ref[1, :, cut]
        first = first + pltpu.roll(first, 7, 0)
        second = second + pltpu.roll(second, 1, 0)
        both = jnp.where(row % 2 == 0, first, second) * factor_ref[6, :, cut]
        for target in range(start // share, (start + LANES) // share):
            energy_ref[target] = both


def inverse_kernel(
    fields, wave_count, points_ref, waves_ref, got_ref, terms_ref, out_ref, energy_ref,
    cos_ref, sin_ref, base_ref, moved, rows_ref, values_ref,
):
    devices, comps = got_ref.shape[0], got_ref.shape[1]
    longitudes = out_ref.shape[1]
    series = comps // 2
    for group in range(devices // LATS):
        cut = pl.ds(group * LANES, LANES)
        for start in range(0, comps, 16):
            arrays = exchange(
                [
                    got_ref[group * LATS + place, pl.ds(start, 16), :].astype(jnp.float32)
                    for place in range(LATS)
                ],
                1,
            )
            for lat, value in enumerate(arrays):
                moved[pl.ds(lat * comps + start, 16), cut] = value.astype(jnp.bfloat16)
    select = select_matrix(waves_ref[...], wave_count)
    rows = lax.dot_general(
        moved[...], select, (((1,), (1,)), ((), ())), preferred_element_type=jnp.float32
    )
    for block in range(rows_ref.shape[0]):
        rows_ref[block] = rows[:, block * LANES : (block + 1) * LANES]
    position = lax.broadcasted_iota(jnp.int32, (series, longitudes), 1)
    wave = lax.broadcasted_iota(jnp.int32, (series, wave_count), 1)

    def one_lat(lat, carry):
        points = points_ref[lat]
        count = points.astype(jnp.float32)
        inverse = 1.0 / jnp.full((1, longitudes), count, jnp.float32)
        fill_tables(count, inverse, cos_ref, sin_ref, base_ref)
        factor = jnp.where(wave < (points + 1) // 2, jnp.where(wave == 0, 1.0, 2.0), 0.0)
        start = lat * comps
        first = (strided_rows(rows_ref, start, series, 2) * factor).astype(jnp.bfloat16)
        second = (strided_rows(rows_ref, start + 1, series, 2) * factor).astype(jnp.bfloat16)
        values = jnp.dot(first, cos_ref[...], preferred_element_type=jnp.float32) - jnp.dot(
            second, sin_ref[...], preferred_element_type=jnp.float32
        )
        values = jnp.where(position < points, values, 0.0)
        store_strided(values_ref, lat, series, LATS, values)
        return carry

    lax.fori_loop(0, LATS, one_lat, 0)
    tendency_out(values_ref, out_ref, fields)

    energy = terms_ref[0]
    for source in range(1, devices):
        energy = energy + terms_ref[source]
    share = wave_count // devices
    device = lax.axis_index("wide") * 2 + lax.axis_index("lev")
    energy = pltpu.roll(energy, lax.rem(LANES - lax.rem(device * share, LANES), LANES), 1)
    for lev in range(2):
        for level in range(4):
            energy_ref[lev * 4 + level : lev * 4 + level + 1, :] = energy[
                2 * level + lev : 2 * level + lev + 1, :share
            ]


def vmem():
    return pl.BlockSpec(memory_space=pltpu.VMEM)


def smem():
    return pl.BlockSpec(memory_space=pltpu.SMEM)


def body(
    model_state, grid_points, quad_weights, slot_waves, legendre, mode_in, mode_out, mode_rates
):
    fields, lev_local, lat_local, longitudes = model_state.shape
    slots, wave_count, lat_all = legendre.shape
    devices = lax.axis_size("wide") * lax.axis_size("lev")
    comps = 2 * fields * lev_local
    assert (lev_local, lat_local, lax.axis_size("lev")) == (4, LATS, 2)
    params = pltpu.CompilerParams(vmem_limit_bytes=VMEM)
    f32, bf16 = jnp.float32, jnp.bfloat16
    blocks = jax.ShapeDtypeStruct((devices, comps, LANES), bf16)
    terms = jax.ShapeDtypeStruct((devices, 8, LANES), f32)

    waves = slot_waves.reshape(devices // LATS, LATS, slots)
    waves = jnp.pad(waves, ((0, 0), (0, 0), (0, PAD_SLOTS - slots)), constant_values=-1)
    waves = jnp.transpose(waves, (0, 2, 1)).reshape(1, devices * PAD_SLOTS)
    places = waves.shape[1]

    sent = pl.pallas_call(
        partial(forward_kernel, fields, wave_count),
        out_shape=blocks,
        in_specs=[smem(), smem(), vmem(), vmem()],
        out_specs=vmem(),
        scratch_shapes=[
            pltpu.VMEM((longitudes // LANES, fields * lev_local * lat_local, LANES), f32),
            pltpu.VMEM((longitudes, wave_count), bf16),
            pltpu.VMEM((longitudes, wave_count), bf16),
            pltpu.VMEM((2, 16 + longitudes // 16, wave_count), f32),
            pltpu.VMEM((wave_count // LANES, lat_local * comps, LANES), f32),
            pltpu.VMEM((lat_local * comps, places), f32),
        ],
        compiler_params=params,
    )(grid_points, quad_weights, model_state.reshape(-1, longitudes), waves)
    got = lax.all_to_all(sent, ("wide", "lev"), split_axis=0, concat_axis=0, tiled=True)

    back, energy_terms = pl.pallas_call(
        partial(spectral_kernel, slots),
        out_shape=(blocks, terms),
        in_specs=[smem(), smem(), smem(), smem(), vmem(), vmem()],
        out_specs=(vmem(), vmem()),
        scratch_shapes=[
            pltpu.VMEM((slots, 2 * comps, lat_all), bf16),
            pltpu.VMEM((32, 8, LANES), f32),
            pltpu.VMEM((7, 8, wave_count), f32),
            pltpu.VMEM((2 * comps, wave_count), bf16),
            pltpu.VMEM((slots, 2 * comps, lat_all), f32),
            pltpu.VMEM((2, 8, wave_count), f32),
        ],
        compiler_params=params,
    )(slot_waves, mode_in, mode_out, mode_rates, got, legendre)
    arrived = lax.all_to_all(back, ("wide", "lev"), split_axis=0, concat_axis=0, tiled=True)
    parts = lax.all_to_all(energy_terms, ("wide", "lev"), split_axis=0, concat_axis=0, tiled=True)

    new_state, energy = pl.pallas_call(
        partial(inverse_kernel, fields, wave_count),
        out_shape=(
            jax.ShapeDtypeStruct((fields * lev_local * lat_local, longitudes), f32),
            jax.ShapeDtypeStruct((8, wave_count // devices), f32),
        ),
        in_specs=[smem(), vmem(), vmem(), vmem()],
        out_specs=(vmem(), vmem()),
        scratch_shapes=[
            pltpu.VMEM((wave_count, longitudes), bf16),
            pltpu.VMEM((wave_count, longitudes), bf16),
            pltpu.VMEM((2, 16 + wave_count // 16, longitudes), f32),
            pltpu.VMEM((lat_local * comps, places), bf16),
            pltpu.VMEM((wave_count // LANES, lat_local * comps, LANES), f32),
            pltpu.VMEM((longitudes // LANES, fields * lev_local * lat_local, LANES), f32),
        ],
        compiler_params=params,
    )(grid_points, waves, arrived, parts)
    return (new_state.reshape(model_state.shape), energy)


def solution(mesh):
    return jax.shard_map(
        body,
        mesh=mesh,
        in_specs=(
            P("ens", "lev", "wide", None),
            P("wide"),
            P("wide"),
            P(),
            P(("wide", "lev"), None, None),
            P(),
            P(),
            P(),
        ),
        out_specs=(P("ens", "lev", "wide", None), P("ens", ("wide", "lev"))),
        check_vma=False,
    )
```

```python
from functools import partial
import math

import jax
import jax.numpy as jnp
from jax import lax
from jax.experimental import pallas as pl
from jax.experimental.pallas import tpu as pltpu
from jax.sharding import PartitionSpec as P

LANES = 128
PAD_SLOTS = 16
LATS = 8
VMEM = 40 * 1024 * 1024


def exchange(arrays, stride):
    lane = lax.broadcasted_iota(jnp.int32, arrays[0].shape, 1)
    arrays = list(arrays)
    step = 1
    while step < len(arrays):
        shift = step * stride
        upper = (lane & shift) != 0
        for low in range(len(arrays)):
            if low & step:
                continue
            first, second = arrays[low], arrays[low | step]
            arrays[low] = jnp.where(upper, pltpu.roll(second, shift, 1), first)
            arrays[low | step] = jnp.where(upper, second, pltpu.roll(first, LANES - shift, 1))
        step *= 2
    return arrays


def turn_pair(product, points, inverse):
    turns = jnp.floor(product * inverse + 0.5)
    half = (product - turns * points) * inverse * math.pi
    square = half * half
    cosine = 1.0 / 479001600.0
    for term in (-1.0 / 3628800.0, 1.0 / 40320.0, -1.0 / 720.0, 1.0 / 24.0, -0.5, 1.0):
        cosine = cosine * square + term
    sine = 1.0 / 6227020800.0
    for term in (-1.0 / 39916800.0, 1.0 / 362880.0, -1.0 / 5040.0, 1.0 / 120.0, -1.0 / 6.0, 1.0):
        sine = sine * square + term
    sine = sine * half
    return (1.0 - 2.0 * sine * sine, 2.0 * sine * cosine)


def fill_tables(points, inverse, cos_ref, sin_ref, base_ref):
    rows, lanes = cos_ref.shape
    highs = rows // 16
    row = lax.broadcasted_iota(jnp.int32, (16 + highs, lanes), 0)
    lane = lax.broadcasted_iota(jnp.int32, (16 + highs, lanes), 1)
    number = jnp.where(row < 16, row, (row - 16) * 16)
    cosine, sine = turn_pair((number * lane).astype(jnp.float32), points, inverse)
    base_ref[0] = cosine
    base_ref[1] = sine
    width = 256
    for start in range(0, lanes, width):
        cut = pl.ds(start, width)
        low_cos = base_ref[0, 0:16, cut]
        low_sin = base_ref[1, 0:16, cut]
        for high in range(highs):
            high_cos = base_ref[0, 16 + high : 17 + high, cut]
            high_sin = base_ref[1, 16 + high : 17 + high, cut]
            place = pl.ds(high * 16, 16)
            cos_ref[place, cut] = (high_cos * low_cos - high_sin * low_sin).astype(jnp.bfloat16)
            sin_ref[place, cut] = (high_sin * low_cos + high_cos * low_sin).astype(jnp.bfloat16)


def strided_rows(ref, start, count, stride):
    place = pl.ds(start, count, stride=stride) if stride else slice(None)
    return jnp.concatenate([ref[block, place, :] for block in range(ref.shape[0])], axis=1)


def store_strided(ref, start, count, stride, value):
    place = pl.ds(start, count, stride=stride)
    for block in range(ref.shape[0]):
        ref[block, place, :] = value[:, block * LANES : (block + 1) * LANES]


def tendency_tile(read, write, rows, fields):
    for start in range(0, rows // fields, 8):
        diverge = read(pl.ds(start, 8))
        for field in range(fields):
            place = pl.ds(field * (rows // fields) + start, 8)
            value = read(place)
            write(place, value - 0.25 * value * diverge)


def tendency_in(source, target, fields):
    for block in range(target.shape[0]):
        cut = pl.ds(block * LANES, LANES)

        def write(place, value):
            target[block, place, :] = value

        tendency_tile(lambda place: source[place, cut], write, source.shape[0], fields)


def tendency_out(source, target, fields):
    for block in range(source.shape[0]):
        cut = pl.ds(block * LANES, LANES)

        def write(place, value):
            target[place, cut] = value

        tendency_tile(lambda place: source[block, place, :], write, target.shape[0], fields)


def select_matrix(waves, wave_count):
    row = lax.broadcasted_iota(jnp.int32, (wave_count, waves.shape[1]), 0)
    return jnp.where(row == waves, 1.0, 0.0).astype(jnp.bfloat16)


def forward_kernel(
    fields, wave_count, points_ref, weight_ref, state_ref, waves_ref, out_ref,
    explicit, cos_ref, sin_ref, base_ref, rows_ref, moved,
):
    longitudes = state_ref.shape[1]
    series = state_ref.shape[0] // LATS
    comps = 2 * series
    tendency_in(state_ref, explicit, fields)
    position = lax.broadcasted_iota(jnp.int32, (series, longitudes), 1)
    wave = lax.broadcasted_iota(jnp.int32, (series, wave_count), 1)

    def one_lat(lat, carry):
        points = points_ref[lat]
        count = points.astype(jnp.float32)
        inverse = 1.0 / jnp.full((1, wave_count), count, jnp.float32)
        fill_tables(count, inverse, cos_ref, sin_ref, base_ref)
        data = strided_rows(explicit, lat, series, LATS)
        data = jnp.where(position < points, data, 0.0).astype(jnp.bfloat16)
        scale = jnp.where(wave < (points + 1) // 2, inverse * weight_ref[lat], 0.0)
        first = jnp.dot(data, cos_ref[...], preferred_element_type=jnp.float32)
        second = jnp.dot(data, sin_ref[...], preferred_element_type=jnp.float32)
        start = lat * comps
        store_strided(rows_ref, start, series, 2, first * scale)
        store_strided(rows_ref, start + 1, series, 2, -second * scale)
        return carry

    lax.fori_loop(0, LATS, one_lat, 0)
    select = select_matrix(waves_ref[...], wave_count)
    rows = strided_rows(rows_ref, 0, rows_ref.shape[1], None).astype(jnp.bfloat16)
    moved[...] = jnp.dot(rows, select, preferred_element_type=jnp.float32)
    for group in range(moved.shape[1] // LANES):
        cut = pl.ds(group * LANES, LANES)
        for start in range(0, comps, 16):
            arrays = exchange(
                [moved[pl.ds(lat * comps + start, 16), cut] for lat in range(LATS)], 1
            )
            for place, value in enumerate(arrays):
                out_ref[group * LATS + place, pl.ds(start, 16), :] = value.astype(jnp.bfloat16)


def mix_weights(matrix_ref, row):
    pairs = {}
    for target in range(2):
        for source in range(2):
            for shift in range(4):
                value = jnp.zeros(row.shape, jnp.float32)
                for mode in range(4):
                    scalar = matrix_ref[target * 4 + mode, source * 4 + (mode - shift) % 4]
                    value = jnp.where(row // 2 == mode, scalar, value)
                pairs[target, source, shift] = value
    return pairs


def mix(weights_ref, which, tiles):
    shifted = [
        [tile if shift == 0 else pltpu.roll(tile, 2 * shift, 0) for shift in range(4)]
        for tile in tiles
    ]
    results = []
    for target in range(2):
        total = None
        for source in range(2):
            for shift in range(4):
                weight = weights_ref[which * 16 + target * 8 + source * 4 + shift]
                term = weight * shifted[source][shift]
                total = term if total is None else total + term
        results.append(total)
    return results


def spectral_kernel(
    slots, waves_ref, mode_in_ref, mode_out_ref, rates_ref, got_ref, legendre_ref,
    out_ref, energy_ref, rows_ref, weights_ref, factor_ref, packed_ref, back_ref, total_ref,
):
    devices, comps = got_ref.shape[0], got_ref.shape[1]
    wide = devices // 2
    wave_count = legendre_ref.shape[1]
    device = lax.axis_index("wide") * 2 + lax.axis_index("lev")
    row = lax.broadcasted_iota(jnp.int32, (8, LANES), 0)
    for which, matrix_ref in enumerate((mode_in_ref, mode_out_ref)):
        for (target, source, shift), value in mix_weights(matrix_ref, row).items():
            weights_ref[which * 16 + target * 8 + source * 4 + shift] = value
    degree = lax.broadcasted_iota(jnp.int32, (8, wave_count), 1).astype(jnp.float32)
    laplace = degree * (degree + 1.0) / (wave_count * wave_count)
    wide_row = lax.broadcasted_iota(jnp.int32, (8, wave_count), 0)
    for target in range(2):
        rate = jnp.zeros((8, wave_count), jnp.float32)
        for mode in range(4):
            rate = jnp.where(wide_row // 2 == mode, rates_ref[target * 4 + mode], rate)
        factor_ref[target] = 1.0 / (1.0 + 4.0 * laplace * rate)
        factor_ref[2 + target] = 2.0 * rate
    factor_ref[4] = 2.0 * laplace
    factor_ref[5] = 1.0 / (1.0 + 8.0 * laplace * laplace)
    factor_ref[6] = wave_count / (degree + 1.0)
    total_ref[...] = jnp.zeros_like(total_ref)

    for lev in range(2):
        for start in range(0, comps, 16):
            place = pl.ds(lev * comps + start, 16)
            for group in range(wide // PAD_SLOTS):
                arrays = exchange(
                    [
                        got_ref[(group * PAD_SLOTS + w) * 2 + lev, pl.ds(start, 16), :].astype(
                            jnp.float32
                        )
                        for w in range(PAD_SLOTS)
                    ],
                    LATS,
                )
                for slot in range(slots):
                    rows_ref[slot, place, pl.ds(group * LANES, LANES)] = arrays[slot].astype(
                        jnp.bfloat16
                    )

    def one_slot(slot, carry):
        spectral = lax.dot_general(
            rows_ref[slot], legendre_ref[slot], (((1,), (1,)), ((), ())),
            preferred_element_type=jnp.float32,
        )
        own_wave = waves_ref[device * slots + slot]
        for start in range(0, wave_count, LANES):
            cut = pl.ds(start, LANES)
            lane = lax.broadcasted_iota(jnp.int32, (8, LANES), 1) + start
            kept = lane >= own_wave

            def tile(lev, index):
                first = lev * comps + index * 8
                return jnp.where(kept, spectral[first : first + 8, start : start + LANES], 0.0)

            div_modes = mix(weights_ref, 0, [tile(lev, 0) for lev in range(2)])
            geo_modes = mix(weights_ref, 0, [tile(lev, 1) for lev in range(2)])
            twice = factor_ref[4, :, cut]
            div_next = [
                (div_modes[lev] + twice * geo_modes[lev]) * factor_ref[lev, :, cut]
                for lev in range(2)
            ]
            geo_next = [
                geo_modes[lev] - factor_ref[2 + lev, :, cut] * div_next[lev] for lev in range(2)
            ]
            div_level = mix(weights_ref, 1, div_next)
            geo_level = mix(weights_ref, 1, geo_next)
            damp = factor_ref[5, :, cut]
            for lev in range(2):
                total_ref[lev, :, cut] += div_level[lev] * div_level[lev]
                tiles = [div_level[lev], geo_level[lev]] + [
                    tile(lev, index) * damp for index in range(2, comps // 8)
                ]
                for index in range(0, comps // 8, 2):
                    packed_ref[pl.ds(lev * comps + index * 8, 16), cut] = jnp.concatenate(
                        tiles[index : index + 2], axis=0
                    ).astype(jnp.bfloat16)
        back_ref[slot] = jnp.dot(
            packed_ref[...], legendre_ref[slot], preferred_element_type=jnp.float32
        )
        return carry

    lax.fori_loop(0, slots, one_slot, 0)

    for lev in range(2):
        for start in range(0, comps, 16):
            place = pl.ds(lev * comps + start, 16)
            for group in range(wide // PAD_SLOTS):
                arrays = exchange(
                    [
                        back_ref[slot, place, pl.ds(group * LANES, LANES)]
                        if slot < slots
                        else jnp.zeros((16, LANES), jnp.float32)
                        for slot in range(PAD_SLOTS)
                    ],
                    LATS,
                )
                for w in range(PAD_SLOTS):
                    out_ref[(group * PAD_SLOTS + w) * 2 + lev, pl.ds(start, 16), :] = arrays[
                        w
                    ].astype(jnp.bfloat16)

    share = wave_count // devices
    for start in range(0, wave_count, LANES):
        cut = pl.ds(start, LANES)
        first, second = total_ref[0, :, cut], total_ref[1, :, cut]
        first = first + pltpu.roll(first, 7, 0)
        second = second + pltpu.roll(second, 1, 0)
        both = jnp.where(row % 2 == 0, first, second) * factor_ref[6, :, cut]
        for target in range(start // share, (start + LANES) // share):
            energy_ref[target] = both


def inverse_kernel(
    fields, wave_count, points_ref, waves_ref, got_ref, terms_ref, out_ref, energy_ref,
    cos_ref, sin_ref, base_ref, moved, rows_ref, values_ref,
):
    devices, comps = got_ref.shape[0], got_ref.shape[1]
    longitudes = out_ref.shape[1]
    series = comps // 2
    for group in range(devices // LATS):
        cut = pl.ds(group * LANES, LANES)
        for start in range(0, comps, 16):
            arrays = exchange(
                [
                    got_ref[group * LATS + place, pl.ds(start, 16), :].astype(jnp.float32)
                    for place in range(LATS)
                ],
                1,
            )
            for lat, value in enumerate(arrays):
                moved[pl.ds(lat * comps + start, 16), cut] = value.astype(jnp.bfloat16)
    select = select_matrix(waves_ref[...], wave_count)
    rows = lax.dot_general(
        moved[...], select, (((1,), (1,)), ((), ())), preferred_element_type=jnp.float32
    )
    for block in range(rows_ref.shape[0]):
        rows_ref[block] = rows[:, block * LANES : (block + 1) * LANES]
    position = lax.broadcasted_iota(jnp.int32, (series, longitudes), 1)
    wave = lax.broadcasted_iota(jnp.int32, (series, wave_count), 1)

    def one_lat(lat, carry):
        points = points_ref[lat]
        count = points.astype(jnp.float32)
        inverse = 1.0 / jnp.full((1, longitudes), count, jnp.float32)
        fill_tables(count, inverse, cos_ref, sin_ref, base_ref)
        factor = jnp.where(wave < (points + 1) // 2, jnp.where(wave == 0, 1.0, 2.0), 0.0)
        start = lat * comps
        first = (strided_rows(rows_ref, start, series, 2) * factor).astype(jnp.bfloat16)
        second = (strided_rows(rows_ref, start + 1, series, 2) * factor).astype(jnp.bfloat16)
        values = jnp.dot(first, cos_ref[...], preferred_element_type=jnp.float32) - jnp.dot(
            second, sin_ref[...], preferred_element_type=jnp.float32
        )
        values = jnp.where(position < points, values, 0.0)
        store_strided(values_ref, lat, series, LATS, values)
        return carry

    lax.fori_loop(0, LATS, one_lat, 0)
    tendency_out(values_ref, out_ref, fields)

    energy = terms_ref[0]
    for source in range(1, devices):
        energy = energy + terms_ref[source]
    share = wave_count // devices
    device = lax.axis_index("wide") * 2 + lax.axis_index("lev")
    energy = pltpu.roll(energy, lax.rem(LANES - lax.rem(device * share, LANES), LANES), 1)
    for lev in range(2):
        for level in range(4):
            energy_ref[lev * 4 + level : lev * 4 + level + 1, :] = energy[
                2 * level + lev : 2 * level + lev + 1, :share
            ]


def vmem():
    return pl.BlockSpec(memory_space=pltpu.VMEM)


def smem():
    return pl.BlockSpec(memory_space=pltpu.SMEM)


def swap_kernel(devices, count, *refs):
    sources, targets = refs[:count], refs[count : 2 * count]
    send_sem, recv_sem, own_sem = refs[2 * count :]
    me = lax.axis_index("wide") * 2 + lax.axis_index("lev")

    def place(peer):
        return {"wide": peer // 2, "lev": lax.rem(peer, 2)}

    barrier = pltpu.get_barrier_semaphore()

    def greet(offset, carry):
        peer = lax.rem(me + offset, devices)
        pl.semaphore_signal(
            barrier, inc=1, device_id=place(peer), device_id_type=pl.DeviceIdType.MESH
        )
        return carry

    lax.fori_loop(1, devices, greet, 0)
    own = [
        pltpu.make_async_copy(sources[k].at[me], targets[k].at[me], own_sem.at[k])
        for k in range(count)
    ]
    for copy in own:
        copy.start()
    pl.semaphore_wait(barrier, devices - 1)

    def copies(offset):
        peer = lax.rem(me + offset, devices)
        return [
            pltpu.make_async_remote_copy(
                src_ref=sources[k].at[peer],
                dst_ref=targets[k].at[me],
                send_sem=send_sem.at[k, offset],
                recv_sem=recv_sem.at[k, offset],
                device_id=place(peer),
                device_id_type=pl.DeviceIdType.MESH,
            )
            for k in range(count)
        ]

    def send(offset, carry):
        for copy in copies(offset):
            copy.start()
        return carry

    def finish(offset, carry):
        for copy in copies(offset):
            copy.wait()
        return carry

    lax.fori_loop(1, devices, send, 0)
    lax.fori_loop(1, devices, finish, 0)
    for copy in own:
        copy.wait()


def swap(arrays, devices, collective):
    count = len(arrays)
    return pl.pallas_call(
        partial(swap_kernel, devices, count),
        out_shape=tuple(jax.ShapeDtypeStruct(a.shape, a.dtype) for a in arrays),
        in_specs=[vmem()] * count,
        out_specs=(vmem(),) * count,
        scratch_shapes=[
            pltpu.SemaphoreType.DMA((count, devices)),
            pltpu.SemaphoreType.DMA((count, devices)),
            pltpu.SemaphoreType.DMA((count,)),
        ],
        compiler_params=pltpu.CompilerParams(
            vmem_limit_bytes=VMEM, collective_id=collective, has_side_effects=True
        ),
    )(*arrays)


def body(
    model_state, grid_points, quad_weights, slot_waves, legendre, mode_in, mode_out, mode_rates
):
    fields, lev_local, lat_local, longitudes = model_state.shape
    slots, wave_count, lat_all = legendre.shape
    devices = lax.axis_size("wide") * lax.axis_size("lev")
    comps = 2 * fields * lev_local
    assert (lev_local, lat_local, lax.axis_size("lev")) == (4, LATS, 2)
    params = pltpu.CompilerParams(vmem_limit_bytes=VMEM)
    f32, bf16 = jnp.float32, jnp.bfloat16
    blocks = jax.ShapeDtypeStruct((devices, comps, LANES), bf16)
    terms = jax.ShapeDtypeStruct((devices, 8, LANES), f32)

    waves = slot_waves.reshape(devices // LATS, LATS, slots)
    waves = jnp.pad(waves, ((0, 0), (0, 0), (0, PAD_SLOTS - slots)), constant_values=-1)
    waves = jnp.transpose(waves, (0, 2, 1)).reshape(1, devices * PAD_SLOTS)
    places = waves.shape[1]

    sent = pl.pallas_call(
        partial(forward_kernel, fields, wave_count),
        out_shape=blocks,
        in_specs=[smem(), smem(), vmem(), vmem()],
        out_specs=vmem(),
        scratch_shapes=[
            pltpu.VMEM((longitudes // LANES, fields * lev_local * lat_local, LANES), f32),
            pltpu.VMEM((longitudes, wave_count), bf16),
            pltpu.VMEM((longitudes, wave_count), bf16),
            pltpu.VMEM((2, 16 + longitudes // 16, wave_count), f32),
            pltpu.VMEM((wave_count // LANES, lat_local * comps, LANES), f32),
            pltpu.VMEM((lat_local * comps, places), f32),
        ],
        compiler_params=params,
    )(grid_points, quad_weights, model_state.reshape(-1, longitudes), waves)
    (got,) = swap([sent], devices, 0)

    back, energy_terms = pl.pallas_call(
        partial(spectral_kernel, slots),
        out_shape=(blocks, terms),
        in_specs=[smem(), smem(), smem(), smem(), vmem(), vmem()],
        out_specs=(vmem(), vmem()),
        scratch_shapes=[
            pltpu.VMEM((slots, 2 * comps, lat_all), bf16),
            pltpu.VMEM((32, 8, LANES), f32),
            pltpu.VMEM((7, 8, wave_count), f32),
            pltpu.VMEM((2 * comps, wave_count), bf16),
            pltpu.VMEM((slots, 2 * comps, lat_all), f32),
            pltpu.VMEM((2, 8, wave_count), f32),
        ],
        compiler_params=params,
    )(slot_waves, mode_in, mode_out, mode_rates, got, legendre)
    arrived, parts = swap([back, energy_terms], devices, 1)

    new_state, energy = pl.pallas_call(
        partial(inverse_kernel, fields, wave_count),
        out_shape=(
            jax.ShapeDtypeStruct((fields * lev_local * lat_local, longitudes), f32),
            jax.ShapeDtypeStruct((8, wave_count // devices), f32),
        ),
        in_specs=[smem(), vmem(), vmem(), vmem()],
        out_specs=(vmem(), vmem()),
        scratch_shapes=[
            pltpu.VMEM((wave_count, longitudes), bf16),
            pltpu.VMEM((wave_count, longitudes), bf16),
            pltpu.VMEM((2, 16 + wave_count // 16, longitudes), f32),
            pltpu.VMEM((lat_local * comps, places), bf16),
            pltpu.VMEM((wave_count // LANES, lat_local * comps, LANES), f32),
            pltpu.VMEM((longitudes // LANES, fields * lev_local * lat_local, LANES), f32),
        ],
        compiler_params=params,
    )(grid_points, waves, arrived, parts)
    return (new_state.reshape(model_state.shape), energy)


def solution(mesh):
    return jax.shard_map(
        body,
        mesh=mesh,
        in_specs=(
            P("ens", "lev", "wide", None),
            P("wide"),
            P("wide"),
            P(),
            P(("wide", "lev"), None, None),
            P(),
            P(),
            P(),
        ),
        out_specs=(P("ens", "lev", "wide", None), P("ens", ("wide", "lev"))),
        check_vma=False,
    )
```

```python
from functools import partial
import math

import jax
import jax.numpy as jnp
from jax import lax
from jax.experimental import pallas as pl
from jax.experimental.pallas import tpu as pltpu
from jax.sharding import PartitionSpec as P

LANES = 128
PAD_SLOTS = 16
LATS = 8
VMEM = 40 * 1024 * 1024


def exchange(arrays, stride):
    lane = lax.broadcasted_iota(jnp.int32, arrays[0].shape, 1)
    arrays = list(arrays)
    step = 1
    while step < len(arrays):
        shift = step * stride
        upper = (lane & shift) != 0
        for low in range(len(arrays)):
            if low & step:
                continue
            first, second = arrays[low], arrays[low | step]
            arrays[low] = jnp.where(upper, pltpu.roll(second, shift, 1), first)
            arrays[low | step] = jnp.where(upper, second, pltpu.roll(first, LANES - shift, 1))
        step *= 2
    return arrays


def turn_pair(product, points, inverse):
    turns = jnp.floor(product * inverse + 0.5)
    half = (product - turns * points) * inverse * math.pi
    square = half * half
    cosine = 1.0 / 479001600.0
    for term in (-1.0 / 3628800.0, 1.0 / 40320.0, -1.0 / 720.0, 1.0 / 24.0, -0.5, 1.0):
        cosine = cosine * square + term
    sine = 1.0 / 6227020800.0
    for term in (-1.0 / 39916800.0, 1.0 / 362880.0, -1.0 / 5040.0, 1.0 / 120.0, -1.0 / 6.0, 1.0):
        sine = sine * square + term
    sine = sine * half
    return (1.0 - 2.0 * sine * sine, 2.0 * sine * cosine)


def fill_tables(points, inverse, cos_ref, sin_ref, base_ref):
    rows, lanes = cos_ref.shape
    highs = rows // 16
    row = lax.broadcasted_iota(jnp.int32, (16 + highs, lanes), 0)
    lane = lax.broadcasted_iota(jnp.int32, (16 + highs, lanes), 1)
    number = jnp.where(row < 16, row, (row - 16) * 16)
    cosine, sine = turn_pair((number * lane).astype(jnp.float32), points, inverse)
    base_ref[0] = cosine
    base_ref[1] = sine
    width = 256
    for start in range(0, lanes, width):
        cut = pl.ds(start, width)
        low_cos = base_ref[0, 0:16, cut]
        low_sin = base_ref[1, 0:16, cut]
        for high in range(highs):
            high_cos = base_ref[0, 16 + high : 17 + high, cut]
            high_sin = base_ref[1, 16 + high : 17 + high, cut]
            place = pl.ds(high * 16, 16)
            cos_ref[place, cut] = (high_cos * low_cos - high_sin * low_sin).astype(jnp.bfloat16)
            sin_ref[place, cut] = (high_sin * low_cos + high_cos * low_sin).astype(jnp.bfloat16)


def strided_rows(ref, start, count, stride):
    place = pl.ds(start, count, stride=stride) if stride else slice(None)
    return jnp.concatenate([ref[block, place, :] for block in range(ref.shape[0])], axis=1)


def store_strided(ref, start, count, stride, value):
    place = pl.ds(start, count, stride=stride)
    for block in range(ref.shape[0]):
        ref[block, place, :] = value[:, block * LANES : (block + 1) * LANES]


def tendency_tile(read, write, rows, fields):
    for start in range(0, rows // fields, 8):
        diverge = read(pl.ds(start, 8))
        for field in range(fields):
            place = pl.ds(field * (rows // fields) + start, 8)
            value = read(place)
            write(place, value - 0.25 * value * diverge)


def tendency_in(source, target, fields):
    for block in range(target.shape[0]):
        cut = pl.ds(block * LANES, LANES)

        def write(place, value):
            target[block, place, :] = value

        tendency_tile(lambda place: source[place, cut], write, source.shape[0], fields)


def tendency_out(source, target, fields):
    for block in range(source.shape[0]):
        cut = pl.ds(block * LANES, LANES)

        def write(place, value):
            target[place, cut] = value

        tendency_tile(lambda place: source[block, place, :], write, target.shape[0], fields)


def select_matrix(waves, wave_count):
    row = lax.broadcasted_iota(jnp.int32, (wave_count, waves.shape[1]), 0)
    return jnp.where(row == waves, 1.0, 0.0).astype(jnp.bfloat16)


def forward_kernel(
    fields, wave_count, points_ref, weight_ref, state_ref, waves_ref, out_ref,
    explicit, cos_ref, sin_ref, base_ref, rows_ref, moved,
):
    longitudes = state_ref.shape[1]
    series = state_ref.shape[0] // LATS
    comps = 2 * series
    tendency_in(state_ref, explicit, fields)
    position = lax.broadcasted_iota(jnp.int32, (series, longitudes), 1)
    wave = lax.broadcasted_iota(jnp.int32, (series, wave_count), 1)

    def one_lat(lat, carry):
        points = points_ref[lat]
        count = points.astype(jnp.float32)
        inverse = 1.0 / jnp.full((1, wave_count), count, jnp.float32)
        fill_tables(count, inverse, cos_ref, sin_ref, base_ref)
        data = strided_rows(explicit, lat, series, LATS)
        data = jnp.where(position < points, data, 0.0).astype(jnp.bfloat16)
        scale = jnp.where(wave < (points + 1) // 2, inverse * weight_ref[lat], 0.0)
        first = jnp.dot(data, cos_ref[...], preferred_element_type=jnp.float32)
        second = jnp.dot(data, sin_ref[...], preferred_element_type=jnp.float32)
        start = lat * comps
        store_strided(rows_ref, start, series, 2, first * scale)
        store_strided(rows_ref, start + 1, series, 2, -second * scale)
        return carry

    lax.fori_loop(0, LATS, one_lat, 0)
    select = select_matrix(waves_ref[...], wave_count)
    rows = strided_rows(rows_ref, 0, rows_ref.shape[1], None).astype(jnp.bfloat16)
    moved[...] = jnp.dot(rows, select, preferred_element_type=jnp.float32)
    for group in range(moved.shape[1] // LANES):
        cut = pl.ds(group * LANES, LANES)
        for start in range(0, comps, 16):
            arrays = exchange(
                [moved[pl.ds(lat * comps + start, 16), cut] for lat in range(LATS)], 1
            )
            for place, value in enumerate(arrays):
                out_ref[group * LATS + place, pl.ds(start, 16), :] = value.astype(jnp.bfloat16)


def mix_weights(matrix_ref, row):
    pairs = {}
    for target in range(2):
        for source in range(2):
            for shift in range(4):
                value = jnp.zeros(row.shape, jnp.float32)
                for mode in range(4):
                    scalar = matrix_ref[target * 4 + mode, source * 4 + (mode - shift) % 4]
                    value = jnp.where(row // 2 == mode, scalar, value)
                pairs[target, source, shift] = value
    return pairs


def mix(weights_ref, which, tiles):
    shifted = [
        [tile if shift == 0 else pltpu.roll(tile, 2 * shift, 0) for shift in range(4)]
        for tile in tiles
    ]
    results = []
    for target in range(2):
        total = None
        for source in range(2):
            for shift in range(4):
                weight = weights_ref[which * 16 + target * 8 + source * 4 + shift]
                term = weight * shifted[source][shift]
                total = term if total is None else total + term
        results.append(total)
    return results


def spectral_kernel(
    slots, waves_src, mode_in_src, mode_out_src, rates_src, got_ref, legendre_src,
    out_ref, energy_ref, rows_ref, weights_ref, factor_ref, packed_ref, back_ref, total_ref,
    waves_ref, mode_in_ref, mode_out_ref, rates_ref, legendre_ref, sems,
):
    pairs = (
        (mode_in_src, mode_in_ref), (mode_out_src, mode_out_ref), (rates_src, rates_ref),
        (waves_src, waves_ref), (legendre_src, legendre_ref),
    )
    loads = [
        pltpu.make_async_copy(source, target, sems.at[k])
        for k, (source, target) in enumerate(pairs)
    ]
    for load in loads:
        load.start()
    for load in loads[:4]:
        load.wait()
    devices, comps = got_ref.shape[0], got_ref.shape[1]
    wide = devices // 2
    wave_count = legendre_ref.shape[1]
    device = lax.axis_index("wide") * 2 + lax.axis_index("lev")
    row = lax.broadcasted_iota(jnp.int32, (8, LANES), 0)
    for which, matrix_ref in enumerate((mode_in_ref, mode_out_ref)):
        for (target, source, shift), value in mix_weights(matrix_ref, row).items():
            weights_ref[which * 16 + target * 8 + source * 4 + shift] = value
    degree = lax.broadcasted_iota(jnp.int32, (8, wave_count), 1).astype(jnp.float32)
    laplace = degree * (degree + 1.0) / (wave_count * wave_count)
    wide_row = lax.broadcasted_iota(jnp.int32, (8, wave_count), 0)
    for target in range(2):
        rate = jnp.zeros((8, wave_count), jnp.float32)
        for mode in range(4):
            rate = jnp.where(wide_row // 2 == mode, rates_ref[target * 4 + mode], rate)
        factor_ref[target] = 1.0 / (1.0 + 4.0 * laplace * rate)
        factor_ref[2 + target] = 2.0 * rate
    factor_ref[4] = 2.0 * laplace
    factor_ref[5] = 1.0 / (1.0 + 8.0 * laplace * laplace)
    factor_ref[6] = wave_count / (degree + 1.0)
    total_ref[...] = jnp.zeros_like(total_ref)

    for lev in range(2):
        for start in range(0, comps, 16):
            place = pl.ds(lev * comps + start, 16)
            for group in range(wide // PAD_SLOTS):
                arrays = exchange(
                    [
                        got_ref[(group * PAD_SLOTS + w) * 2 + lev, pl.ds(start, 16), :].astype(
                            jnp.float32
                        )
                        for w in range(PAD_SLOTS)
                    ],
                    LATS,
                )
                for slot in range(slots):
                    rows_ref[slot, place, pl.ds(group * LANES, LANES)] = arrays[slot].astype(
                        jnp.bfloat16
                    )

    loads[4].wait()

    def one_slot(slot, carry):
        spectral = lax.dot_general(
            rows_ref[slot], legendre_ref[slot], (((1,), (1,)), ((), ())),
            preferred_element_type=jnp.float32,
        )
        own_wave = waves_ref[device * slots + slot]
        for start in range(0, wave_count, LANES):
            cut = pl.ds(start, LANES)
            lane = lax.broadcasted_iota(jnp.int32, (8, LANES), 1) + start
            kept = lane >= own_wave

            def tile(lev, index):
                first = lev * comps + index * 8
                return jnp.where(kept, spectral[first : first + 8, start : start + LANES], 0.0)

            div_modes = mix(weights_ref, 0, [tile(lev, 0) for lev in range(2)])
            geo_modes = mix(weights_ref, 0, [tile(lev, 1) for lev in range(2)])
            twice = factor_ref[4, :, cut]
            div_next = [
                (div_modes[lev] + twice * geo_modes[lev]) * factor_ref[lev, :, cut]
                for lev in range(2)
            ]
            geo_next = [
                geo_modes[lev] - factor_ref[2 + lev, :, cut] * div_next[lev] for lev in range(2)
            ]
            div_level = mix(weights_ref, 1, div_next)
            geo_level = mix(weights_ref, 1, geo_next)
            damp = factor_ref[5, :, cut]
            for lev in range(2):
                total_ref[lev, :, cut] += div_level[lev] * div_level[lev]
                tiles = [div_level[lev], geo_level[lev]] + [
                    tile(lev, index) * damp for index in range(2, comps // 8)
                ]
                for index in range(0, comps // 8, 2):
                    packed_ref[pl.ds(lev * comps + index * 8, 16), cut] = jnp.concatenate(
                        tiles[index : index + 2], axis=0
                    ).astype(jnp.bfloat16)
        back_ref[slot] = jnp.dot(
            packed_ref[...], legendre_ref[slot], preferred_element_type=jnp.float32
        )
        return carry

    lax.fori_loop(0, slots, one_slot, 0)

    for lev in range(2):
        for start in range(0, comps, 16):
            place = pl.ds(lev * comps + start, 16)
            for group in range(wide // PAD_SLOTS):
                arrays = exchange(
                    [
                        back_ref[slot, place, pl.ds(group * LANES, LANES)]
                        if slot < slots
                        else jnp.zeros((16, LANES), jnp.float32)
                        for slot in range(PAD_SLOTS)
                    ],
                    LATS,
                )
                for w in range(PAD_SLOTS):
                    out_ref[(group * PAD_SLOTS + w) * 2 + lev, pl.ds(start, 16), :] = arrays[
                        w
                    ].astype(jnp.bfloat16)

    share = wave_count // devices
    for start in range(0, wave_count, LANES):
        cut = pl.ds(start, LANES)
        first, second = total_ref[0, :, cut], total_ref[1, :, cut]
        first = first + pltpu.roll(first, 7, 0)
        second = second + pltpu.roll(second, 1, 0)
        both = jnp.where(row % 2 == 0, first, second) * factor_ref[6, :, cut]
        for target in range(start // share, (start + LANES) // share):
            energy_ref[target] = both


def inverse_kernel(
    fields, wave_count, points_ref, waves_ref, got_ref, terms_ref, out_ref, energy_ref,
    cos_ref, sin_ref, base_ref, moved, rows_ref, values_ref,
):
    devices, comps = got_ref.shape[0], got_ref.shape[1]
    longitudes = out_ref.shape[1]
    series = comps // 2
    for group in range(devices // LATS):
        cut = pl.ds(group * LANES, LANES)
        for start in range(0, comps, 16):
            arrays = exchange(
                [
                    got_ref[group * LATS + place, pl.ds(start, 16), :].astype(jnp.float32)
                    for place in range(LATS)
                ],
                1,
            )
            for lat, value in enumerate(arrays):
                moved[pl.ds(lat * comps + start, 16), cut] = value.astype(jnp.bfloat16)
    select = select_matrix(waves_ref[...], wave_count)
    rows = lax.dot_general(
        moved[...], select, (((1,), (1,)), ((), ())), preferred_element_type=jnp.float32
    )
    for block in range(rows_ref.shape[0]):
        rows_ref[block] = rows[:, block * LANES : (block + 1) * LANES]
    position = lax.broadcasted_iota(jnp.int32, (series, longitudes), 1)
    wave = lax.broadcasted_iota(jnp.int32, (series, wave_count), 1)

    def one_lat(lat, carry):
        points = points_ref[lat]
        count = points.astype(jnp.float32)
        inverse = 1.0 / jnp.full((1, longitudes), count, jnp.float32)
        fill_tables(count, inverse, cos_ref, sin_ref, base_ref)
        factor = jnp.where(wave < (points + 1) // 2, jnp.where(wave == 0, 1.0, 2.0), 0.0)
        start = lat * comps
        first = (strided_rows(rows_ref, start, series, 2) * factor).astype(jnp.bfloat16)
        second = (strided_rows(rows_ref, start + 1, series, 2) * factor).astype(jnp.bfloat16)
        values = jnp.dot(first, cos_ref[...], preferred_element_type=jnp.float32) - jnp.dot(
            second, sin_ref[...], preferred_element_type=jnp.float32
        )
        values = jnp.where(position < points, values, 0.0)
        store_strided(values_ref, lat, series, LATS, values)
        return carry

    lax.fori_loop(0, LATS, one_lat, 0)
    tendency_out(values_ref, out_ref, fields)

    energy = terms_ref[0]
    for source in range(1, devices):
        energy = energy + terms_ref[source]
    share = wave_count // devices
    device = lax.axis_index("wide") * 2 + lax.axis_index("lev")
    energy = pltpu.roll(energy, lax.rem(LANES - lax.rem(device * share, LANES), LANES), 1)
    for lev in range(2):
        for level in range(4):
            energy_ref[lev * 4 + level : lev * 4 + level + 1, :] = energy[
                2 * level + lev : 2 * level + lev + 1, :share
            ]


def vmem():
    return pl.BlockSpec(memory_space=pltpu.VMEM)


def anywhere():
    return pl.BlockSpec(memory_space=pl.ANY)


def smem():
    return pl.BlockSpec(memory_space=pltpu.SMEM)


def swap_kernel(devices, count, *refs):
    sources, targets = refs[:count], refs[count : 2 * count]
    send_sem, recv_sem, own_sem = refs[2 * count :]
    me = lax.axis_index("wide") * 2 + lax.axis_index("lev")

    def place(peer):
        return {"wide": peer // 2, "lev": lax.rem(peer, 2)}

    barrier = pltpu.get_barrier_semaphore()

    def greet(offset, carry):
        peer = lax.rem(me + offset, devices)
        pl.semaphore_signal(
            barrier, inc=1, device_id=place(peer), device_id_type=pl.DeviceIdType.MESH
        )
        return carry

    lax.fori_loop(1, devices, greet, 0)
    own = [
        pltpu.make_async_copy(sources[k].at[me], targets[k].at[me], own_sem.at[k])
        for k in range(count)
    ]
    for copy in own:
        copy.start()
    pl.semaphore_wait(barrier, devices - 1)

    def copies(offset):
        peer = lax.rem(me + offset, devices)
        return [
            pltpu.make_async_remote_copy(
                src_ref=sources[k].at[peer],
                dst_ref=targets[k].at[me],
                send_sem=send_sem.at[k, offset],
                recv_sem=recv_sem.at[k, offset],
                device_id=place(peer),
                device_id_type=pl.DeviceIdType.MESH,
            )
            for k in range(count)
        ]

    def send(offset, carry):
        for copy in copies(offset):
            copy.start()
        return carry

    def finish(offset, carry):
        for copy in copies(offset):
            copy.wait()
        return carry

    lax.fori_loop(1, devices, send, 0)
    lax.fori_loop(1, devices, finish, 0)
    for copy in own:
        copy.wait()


def swap(arrays, devices, collective):
    count = len(arrays)
    return pl.pallas_call(
        partial(swap_kernel, devices, count),
        out_shape=tuple(jax.ShapeDtypeStruct(a.shape, a.dtype) for a in arrays),
        in_specs=[vmem()] * count,
        out_specs=(vmem(),) * count,
        scratch_shapes=[
            pltpu.SemaphoreType.DMA((count, devices)),
            pltpu.SemaphoreType.DMA((count, devices)),
            pltpu.SemaphoreType.DMA((count,)),
        ],
        compiler_params=pltpu.CompilerParams(
            vmem_limit_bytes=VMEM, collective_id=collective, has_side_effects=True
        ),
    )(*arrays)


def body(
    model_state, grid_points, quad_weights, slot_waves, legendre, mode_in, mode_out, mode_rates
):
    fields, lev_local, lat_local, longitudes = model_state.shape
    slots, wave_count, lat_all = legendre.shape
    devices = lax.axis_size("wide") * lax.axis_size("lev")
    comps = 2 * fields * lev_local
    assert (lev_local, lat_local, lax.axis_size("lev")) == (4, LATS, 2)
    params = pltpu.CompilerParams(vmem_limit_bytes=VMEM)
    f32, bf16 = jnp.float32, jnp.bfloat16
    blocks = jax.ShapeDtypeStruct((devices, comps, LANES), bf16)
    terms = jax.ShapeDtypeStruct((devices, 8, LANES), f32)

    waves = slot_waves.reshape(devices // LATS, LATS, slots)
    waves = jnp.pad(waves, ((0, 0), (0, 0), (0, PAD_SLOTS - slots)), constant_values=-1)
    waves = jnp.transpose(waves, (0, 2, 1)).reshape(1, devices * PAD_SLOTS)
    places = waves.shape[1]

    sent = pl.pallas_call(
        partial(forward_kernel, fields, wave_count),
        out_shape=blocks,
        in_specs=[smem(), smem(), vmem(), vmem()],
        out_specs=vmem(),
        scratch_shapes=[
            pltpu.VMEM((longitudes // LANES, fields * lev_local * lat_local, LANES), f32),
            pltpu.VMEM((longitudes, wave_count), bf16),
            pltpu.VMEM((longitudes, wave_count), bf16),
            pltpu.VMEM((2, 16 + longitudes // 16, wave_count), f32),
            pltpu.VMEM((wave_count // LANES, lat_local * comps, LANES), f32),
            pltpu.VMEM((lat_local * comps, places), f32),
        ],
        compiler_params=params,
    )(grid_points, quad_weights, model_state.reshape(-1, longitudes), waves)
    (got,) = swap([sent], devices, 0)

    back, energy_terms = pl.pallas_call(
        partial(spectral_kernel, slots),
        out_shape=(blocks, terms),
        in_specs=[anywhere()] * 4 + [vmem(), anywhere()],
        out_specs=(vmem(), vmem()),
        scratch_shapes=[
            pltpu.VMEM((slots, 2 * comps, lat_all), bf16),
            pltpu.VMEM((32, 8, LANES), f32),
            pltpu.VMEM((7, 8, wave_count), f32),
            pltpu.VMEM((2 * comps, wave_count), bf16),
            pltpu.VMEM((slots, 2 * comps, lat_all), f32),
            pltpu.VMEM((2, 8, wave_count), f32),
            pltpu.SMEM(slot_waves.shape, jnp.int32),
            pltpu.SMEM(mode_in.shape, f32),
            pltpu.SMEM(mode_out.shape, f32),
            pltpu.SMEM(mode_rates.shape, f32),
            pltpu.VMEM(legendre.shape, bf16),
            pltpu.SemaphoreType.DMA((5,)),
        ],
        compiler_params=params,
    )(slot_waves, mode_in, mode_out, mode_rates, got, legendre)
    arrived, parts = swap([back, energy_terms], devices, 1)

    new_state, energy = pl.pallas_call(
        partial(inverse_kernel, fields, wave_count),
        out_shape=(
            jax.ShapeDtypeStruct((fields * lev_local * lat_local, longitudes), f32),
            jax.ShapeDtypeStruct((8, wave_count // devices), f32),
        ),
        in_specs=[smem(), vmem(), vmem(), vmem()],
        out_specs=(vmem(), vmem()),
        scratch_shapes=[
            pltpu.VMEM((wave_count, longitudes), bf16),
            pltpu.VMEM((wave_count, longitudes), bf16),
            pltpu.VMEM((2, 16 + wave_count // 16, longitudes), f32),
            pltpu.VMEM((lat_local * comps, places), bf16),
            pltpu.VMEM((wave_count // LANES, lat_local * comps, LANES), f32),
            pltpu.VMEM((longitudes // LANES, fields * lev_local * lat_local, LANES), f32),
        ],
        compiler_params=params,
    )(grid_points, waves, arrived, parts)
    return (new_state.reshape(model_state.shape), energy)


def solution(mesh):
    return jax.shard_map(
        body,
        mesh=mesh,
        in_specs=(
            P("ens", "lev", "wide", None),
            P("wide"),
            P("wide"),
            P(),
            P(("wide", "lev"), None, None),
            P(),
            P(),
            P(),
        ),
        out_specs=(P("ens", "lev", "wide", None), P("ens", ("wide", "lev"))),
        check_vma=False,
    )
```
